32 devices in a mesh: section: 8 (over y, x, core), rep: 4 (over z).
Axes of the slice: x: 2, y: 2, z: 4, core: 2. Of those that a mesh axis runs over, the one named last changes fastest.
Arguments:
- inflow: bfloat16 [8, 4, 4, 16, 3584], P('section', 'rep'), may hold values from -6 to 6
- cotangent: bfloat16 [8, 4, 4, 16, 3584], P('section', 'rep'), may hold values from -0.1796875 to 0.1796875
- reduce_weight: bfloat16 [8, 4, 3584, 192], P('section', 'rep'), may hold values from -0.09375 to 0.09375
- expand_weight: bfloat16 [8, 4, 3584, 192], P('section', 'rep'), may hold values from -0.4375 to 0.4375
- held: int32 [8, 4], replicated, may hold values from 0 to 4, as said below
- routes: int32 [2, 8, 4, 4], replicated, may hold values from 0 to 3, as said below
Outputs:
- reduce_grad: bfloat16 [8, 3584, 192], P('section', 'rep')
- expand_grad: bfloat16 [8, 3584, 192], P('section', 'rep')
The draws below stay inside these ranges and needn't reach their ends.
Inputs may be any that keep to these rules, and one draw needn't show every extreme that they name: Lanes of a device at the first tick sit in slots 0 to held - 1. Sections above 5 hold none; every other section has a replica that holds 4. `routes`: within one section and tick the 4 slots of a device name distinct replicas, and every replica is named by exactly 4 slots of the section, live or not.
All inputs are finite; a program needn't handle non-finite values.
Results may differ from the reference program's by a relative error of at most 0.014.
Values may be sent and summed in bfloat16 or wider, within the bound.
A program may use at most 64 MiB of HBM per device.

```python
import jax
import jax.numpy as jnp
from jax import lax

D = 3584
L = 192
ROWS = 16
TICKS = 3
CAP = 4
N_SECTION = 8
N_REP = 4


def draw_held(key, part):
    key = jax.random.fold_in(key, 11)
    key_counts, key_full = jax.random.split(key)
    counts = jax.random.randint(key_counts, (N_SECTION, N_REP), 0, CAP + 1)
    full_replica = jax.random.randint(key_full, (N_SECTION, 1), 0, N_REP)
    replica_ids = jnp.arange(N_REP)[None, :]
    counts = jnp.where(replica_ids == full_replica, CAP, counts)
    active = jnp.arange(N_SECTION)[:, None] <= N_SECTION - TICKS
    return jnp.where(active, counts, 0).astype(jnp.int32)


def shuffle_slots(key):
    return jax.random.permutation(key, CAP)


def route_group(key):
    subkeys = jax.random.split(key, 4)
    src_order = jax.random.permutation(subkeys[0], N_REP)
    dst_order = jax.random.permutation(subkeys[1], N_REP)
    offsets = jax.random.permutation(subkeys[2], N_REP)[:CAP]
    slot_keys = jax.random.split(subkeys[3], N_REP)
    shuffles = jax.vmap(shuffle_slots)(slot_keys)
    position = (src_order[:, None] + offsets[shuffles]) % N_REP
    return dst_order[position]


def draw_routes(key, part):
    key = jax.random.fold_in(key, 23)
    subkeys = jax.random.split(key, (TICKS - 1) * N_SECTION)
    groups = jax.vmap(route_group)(subkeys)
    return groups.reshape(TICKS - 1, N_SECTION, N_REP, CAP).astype(jnp.int32)


def steps_of(rng, extent, shards, low, top_value):
    gain, own = 1.0, jax.random.fold_in(rng, 6)
    for dim, parts in shards:
        draws = jnp.exp(jax.random.uniform(jax.random.fold_in(own, dim), (parts,), jnp.float32, low / len(shards), top_value / len(shards)))
        gain = gain * jnp.repeat(draws, extent[dim] // parts).reshape([-1 if axis == dim else 1 for axis in range(len(extent))])
    return gain


def scatter_about(own_key, extent, deviation, limit, pieces=(), held_as=jnp.bfloat16):
    array = deviation * jax.random.normal(own_key, extent, jnp.float32)
    if pieces:
        array = array * steps_of(own_key, extent, pieces, -0.22, 0.18)
    return jnp.clip(array, -limit, limit).astype(held_as)


def setup_inputs(seed: int = 0) -> dict:
    key_of = jax.random.split(jax.random.key(seed), 7)
    return {
        "inflow": scatter_about(key_of[0], (N_SECTION, N_REP, CAP, ROWS, D), 1.0, 6.0, ((0, 8), (1, 4))),
        "cotangent": scatter_about(key_of[1], (N_SECTION, N_REP, CAP, ROWS, D), 0.03, 0.1796875, ((0, 8), (1, 4))),
        "reduce_weight": scatter_about(key_of[2], (N_SECTION, N_REP, D, L), D ** -0.5, 0.09375, ((0, 8), (1, 4))),
        "expand_weight": scatter_about(key_of[3], (N_SECTION, N_REP, D, L), L ** -0.5, 0.4375, ((0, 8), (1, 4))),
        "held": draw_held(jax.random.fold_in(key_of[6], 71), 0),
        "routes": draw_routes(jax.random.fold_in(key_of[6], 71), 0),
    }


epsilon = 1e-06

def wiring(counts, targets):
    slot_ids = jnp.arange(CAP, dtype=jnp.int32)
    replica_ids = jnp.arange(N_REP, dtype=jnp.int32)
    slot_live = slot_ids[None, None, :] < counts[:, :, None]
    matched = (slot_live[:, :, :, None] & (targets[:, :, :, None] == replica_ids[None, None, None, :])).astype(jnp.int32)
    pair_sent = lax.optimization_barrier(jnp.sum(matched, axis=2)).astype(jnp.int32)
    pair_slot = lax.optimization_barrier(jnp.sum(matched * slot_ids[None, None, :, None], axis=2)).astype(jnp.int32)
    pair_rank = (jnp.cumsum(pair_sent, axis=1) - pair_sent).astype(jnp.int32)
    arrived = lax.optimization_barrier(jnp.sum(pair_sent, axis=1)).astype(jnp.int32)
    following = jnp.concatenate([jnp.zeros_like(arrived[:1]), arrived[:-1]], axis=0)
    return (slot_live, pair_sent, pair_slot, pair_rank, following)

def layer_parts(current, reduce_w):
    widened = current.astype(jnp.float32)
    inverse_rms = lax.rsqrt(lax.optimization_barrier(jnp.mean(widened * widened, axis=-1, keepdims=True)) + epsilon)
    unit_rows = widened * inverse_rms
    normed = unit_rows.astype(jnp.bfloat16)
    pre_act = jnp.einsum('akrd,adl->akrl', normed.astype(jnp.float32), reduce_w.astype(jnp.float32))
    hidden = jax.nn.silu(pre_act).astype(jnp.bfloat16)
    return (widened, inverse_rms, unit_rows, normed, pre_act, hidden)

def section_forward(operands):
    current, reduce_w, expand_w = operands
    widened, inverse_rms, unit_rows, normed, pre_act, hidden = layer_parts(current, reduce_w)
    branch_out = jnp.einsum('akrl,adl->akrd', hidden.astype(jnp.float32), expand_w.astype(jnp.float32))
    return (widened + branch_out).astype(jnp.bfloat16)

def pre_gradient(upstream, pre_act, expand_w):
    grad_hidden = jnp.einsum('akrd,adl->akrl', upstream.astype(jnp.float32), expand_w.astype(jnp.float32))
    sigmoid_pre = jax.nn.sigmoid(pre_act)
    return (grad_hidden * sigmoid_pre * (1.0 + pre_act * (1.0 - sigmoid_pre))).astype(jnp.bfloat16)

def section_backward(operands):
    current, upstream, reduce_w, expand_w = operands
    widened, inverse_rms, unit_rows, normed, pre_act, hidden = layer_parts(current, reduce_w)
    grad_pre = pre_gradient(upstream, pre_act, expand_w)
    grad_unit = jnp.einsum('akrl,adl->akrd', grad_pre.astype(jnp.float32), reduce_w.astype(jnp.float32))
    inner_term = lax.optimization_barrier(jnp.mean(grad_unit * unit_rows, axis=-1, keepdims=True))
    returned = upstream.astype(jnp.float32) + inverse_rms * (grad_unit - unit_rows * inner_term)
    return returned.astype(jnp.bfloat16)

def forward_move(outputs, pair_sent, pair_slot, pair_rank):
    slot_ids = jnp.arange(CAP, dtype=jnp.int32)
    replica_ids = jnp.arange(N_REP, dtype=jnp.int32)
    chosen = ((pair_sent[:, :, :, None] == 1) & (pair_rank[:, :, :, None] == slot_ids[None, None, None, :])).astype(jnp.int32)
    source_rep = lax.optimization_barrier(jnp.sum(chosen * replica_ids[None, :, None, None], axis=1)).astype(jnp.int32)
    source_slot = lax.optimization_barrier(jnp.sum(chosen * pair_slot[:, :, :, None], axis=1)).astype(jnp.int32)
    present = lax.optimization_barrier(jnp.sum(chosen, axis=1)) == 1
    section_ids = jnp.arange(N_SECTION, dtype=jnp.int32)[:, None, None]
    moved_lanes = outputs[section_ids, source_rep, source_slot]
    moved_lanes = jnp.where(present[:, :, :, None, None], moved_lanes, jnp.zeros_like(moved_lanes))
    return jnp.concatenate([jnp.zeros_like(moved_lanes[:1]), moved_lanes[:-1]], axis=0)

def backward_move(returned, slot_live, targets, pair_rank):
    from_next = jnp.concatenate([returned[1:], jnp.zeros_like(returned[:1])], axis=0)
    arrival = jnp.take_along_axis(pair_rank, targets, axis=2).astype(jnp.int32)
    section_ids = jnp.arange(N_SECTION, dtype=jnp.int32)[:, None, None]
    gathered = from_next[section_ids, targets, arrival]
    return jnp.where(slot_live[:, :, :, None, None], gathered, jnp.zeros_like(gathered))

def reference(inflow, cotangent, reduce_weight, expand_weight, held, routes):
    counts = held
    wirings = []
    for step_index in range(TICKS - 1):
        slot_live, pair_sent, pair_slot, pair_rank, counts = wiring(counts, routes[step_index])
        wirings.append((slot_live, pair_sent, pair_slot, pair_rank))
    slot_ids = jnp.arange(CAP, dtype=jnp.int32)
    first_live = slot_ids[None, None, :] < held[:, :, None]
    last_live = slot_ids[None, None, :] < counts[:, :, None]
    current = jnp.where(first_live[:, :, :, None, None], inflow, jnp.zeros_like(inflow))
    stashed = [current]
    for step_index in range(TICKS - 1):
        outputs = lax.map(section_forward, (current, reduce_weight, expand_weight))
        slot_live, pair_sent, pair_slot, pair_rank = wirings[step_index]
        current = forward_move(outputs, pair_sent, pair_slot, pair_rank)
        stashed.append(current)
    upstream = jnp.where(last_live[:, :, :, None, None], cotangent, jnp.zeros_like(cotangent))
    arriving = [upstream]
    for step_index in range(TICKS - 1, 0, -1):
        returned = lax.map(section_backward, (stashed[step_index], upstream, reduce_weight, expand_weight))
        slot_live, pair_sent, pair_slot, pair_rank = wirings[step_index - 1]
        upstream = backward_move(returned, slot_live, routes[step_index - 1], pair_rank)
        arriving.insert(0, upstream)

    def section_gradients(section_id):
        reduce_w = reduce_weight[section_id]
        expand_w = expand_weight[section_id]
        total_reduce = jnp.zeros((N_REP, D, L), jnp.float32)
        total_expand = jnp.zeros((N_REP, D, L), jnp.float32)
        for step_index in range(TICKS):
            current_rows = stashed[step_index][section_id]
            upstream_rows = arriving[step_index][section_id]
            widened, inverse_rms, unit_rows, normed, pre_act, hidden = layer_parts(current_rows, reduce_w)
            grad_pre = pre_gradient(upstream_rows, pre_act, expand_w)
            total_reduce = total_reduce + jnp.einsum('akrd,akrl->adl', normed.astype(jnp.float32), grad_pre.astype(jnp.float32))
            total_expand = total_expand + jnp.einsum('akrd,akrl->adl', upstream_rows.astype(jnp.float32), hidden.astype(jnp.float32))
        rounded_reduce = lax.optimization_barrier(total_reduce.astype(jnp.bfloat16))
        rounded_expand = lax.optimization_barrier(total_expand.astype(jnp.bfloat16))
        summed_reduce = lax.optimization_barrier(jnp.sum(rounded_reduce.astype(jnp.float32), axis=0)).astype(jnp.bfloat16)
        summed_expand = lax.optimization_barrier(jnp.sum(rounded_expand.astype(jnp.float32), axis=0)).astype(jnp.bfloat16)
        return (summed_reduce, summed_expand)
    reduce_grad, expand_grad = lax.map(section_gradients, jnp.arange(N_SECTION, dtype=jnp.int32))
    return (reduce_grad, expand_grad)
```

```python
import functools

import jax
import jax.numpy as jnp
from jax import lax
from jax.experimental import pallas as pl
from jax.experimental.pallas import tpu as pltpu
from jax.sharding import PartitionSpec as P

TICKS = 3
HOPS = TICKS - 1
EPS = 1e-06
MESH = pl.DeviceIdType.MESH
NT = (((1,), (1,)), ((), ()))
NN = (((1,), (0,)), ((), ()))


def dot(a, b, dims):
    return lax.dot_general(a, b, dims, preferred_element_type=jnp.float32)


def chunks(total, size):
    return [(start, min(size, total - start)) for start in range(0, total, size)]


def kernel(
    sections, n, cap, rows, features, rank,
    held, routes, inflow_hbm, cot_hbm, wr_hbm, we_hbm,
    out,
    inflow, cot, wr, we,
    lanes, landed0, landed1, fwd_out, bwd_out, back, ups, normed, inv, pre, hid, gp,
    part, up_buf, down_buf,
    load_sem, send_sem, recv_sem, bsend_sem, brecv_sem,
    up_send, up_recv, down_send, down_recv,
):
    c = lax.axis_index("section")
    r = lax.axis_index("rep")
    tick_rows = n * rows
    share = features // n
    column_chunks = chunks(features, 512)
    landed = (landed0, landed1)

    loads = [
        pltpu.make_async_copy(src, dst, load_sem.at[i])
        for i, (src, dst) in enumerate(
            [(inflow_hbm, inflow), (wr_hbm, wr), (we_hbm, we), (cot_hbm, cot)]
        )
    ]
    for load in loads:
        load.start()

    barrier = pltpu.get_barrier_semaphore()
    for step in (1, -1):
        other = c + step

        @pl.when((other >= 0) & (other < sections))
        def _():
            for d in range(n):
                pl.semaphore_signal(barrier, inc=1, device_id=(other, d), device_id_type=MESH)

        near = r + step

        @pl.when((near >= 0) & (near < n))
        def _():
            pl.semaphore_signal(barrier, inc=1, device_id=(c, near), device_id_type=MESH)

    def one_if(condition):
        return condition.astype(jnp.int32)

    pl.semaphore_wait(
        barrier,
        n * (one_if(c > 0) + one_if(c < sections - 1)) + one_if(r > 0) + one_if(r < n - 1),
    )

    prev = jnp.maximum(c - 1, 0)
    prev2 = jnp.maximum(c - 2, 0)
    zero = jnp.int32(0)

    def first_tick_sends(section, s, dest):
        def step(k, carry):
            slot, seen = carry
            hit = ((routes[0, section, s, k] == dest) & (k < held[section, s])).astype(jnp.int32)
            return slot + hit * k, seen + hit
        return lax.fori_loop(0, cap, step, (zero, zero), unroll=cap <= 4)

    lane0 = [first_tick_sends(c, r, d) for d in range(n)]
    sent0 = [
        first_tick_sends(prev, s, r)[1] * (c >= 1).astype(jnp.int32) for s in range(n)
    ]

    def ranks(sent):
        total, out_ranks = zero, []
        for s in range(n):
            out_ranks.append(total)
            total = total + sent[s]
        return out_ranks

    rank1 = [jnp.minimum(v, cap - 1) for v in ranks(sent0)]
    dest1 = [routes[1, c, r, rank1[s]] for s in range(n)]
    lane1 = []
    for d in range(n):
        index, seen = zero, zero
        for s in range(n):
            hit = sent0[s] * (dest1[s] == d).astype(jnp.int32)
            index, seen = index + hit * s, seen + hit
        lane1.append((index, seen))

    def count1(s):
        def step(s0, total):
            return total + first_tick_sends(prev2, s0, s)[1]
        return lax.fori_loop(0, n, step, zero, unroll=n <= 4) * (c >= 2).astype(jnp.int32)

    sent1 = []
    for s in range(n):
        count = count1(s)

        def step(k, seen, s=s, count=count):
            return seen + ((routes[1, prev, s, k] == r) & (k < count)).astype(jnp.int32)
        sent1.append(lax.fori_loop(0, cap, step, zero, unroll=cap <= 4))
    rank2 = [jnp.minimum(v, cap - 1) for v in ranks(sent1)]

    def pick(source, index, seen):
        value = source[pl.ds(index, 1)][0]
        return jnp.where(seen > 0, value, jnp.zeros_like(value))

    def live_at(tick, section):
        return (section >= tick) & (section <= sections - TICKS + tick)

    def hop_copies(hop, forward):
        buf = fwd_out if forward else bwd_out
        dst = landed[hop] if forward else ups.at[hop]
        sems = (send_sem, recv_sem) if forward else (bsend_sem, brecv_sem)
        target = c + 1 if forward else c - 1
        return [
            pltpu.make_async_remote_copy(
                src_ref=buf.at[hop, d],
                dst_ref=dst.at[r],
                send_sem=sems[0].at[hop, d],
                recv_sem=sems[1].at[hop, r],
                device_id=(target, d),
                device_id_type=MESH,
            )
            for d in range(n)
        ]

    def await_lanes(hop, forward):
        buf = fwd_out if forward else bwd_out
        dst = landed[hop] if forward else ups.at[hop]
        sems = (send_sem, recv_sem) if forward else (bsend_sem, brecv_sem)
        for s in range(n):
            pltpu.make_async_remote_copy(
                src_ref=buf.at[hop, s],
                dst_ref=dst.at[s],
                send_sem=sems[0].at[hop, s],
                recv_sem=sems[1].at[hop, s],
                device_id=(c, s),
                device_id_type=MESH,
            ).wait_recv()

    def normalise(tick, i, lane):
        lanes[tick, i] = lane
        wide = lane.astype(jnp.float32)
        scale = lax.rsqrt(jnp.mean(wide * wide, axis=-1, keepdims=True) + EPS)
        at = pl.ds(tick * tick_rows + i * rows, rows)
        inv[at, :] = jnp.broadcast_to(scale, (rows, 128))
        normed[at, :] = (wide * scale).astype(jnp.bfloat16)

    def forward(tick):
        at = pl.ds(tick * tick_rows, tick_rows)
        p = dot(normed[at, :], wr[...], NT)
        pre[at, :] = p
        h = (p / (1.0 + jnp.exp(-p))).astype(jnp.bfloat16)
        hid[at, :] = h
        return h

    def emit(tick, h):
        for start, size in column_chunks:
            cols = pl.ds(start, size)
            branch = dot(h, we[:, cols], NN).reshape(n, rows, size)
            fwd_out[tick, :, :, cols] = (
                lanes[tick, :, :, cols].astype(jnp.float32) + branch
            ).astype(jnp.bfloat16)

        @pl.when(live_at(tick, c))
        def _():
            for copy in hop_copies(tick, True):
                copy.start()

    def receive(hop, forward, tick):
        dst = landed[hop] if forward else ups.at[hop]

        @pl.when(live_at(tick, c))
        def _():
            await_lanes(hop, forward)

        @pl.when(jnp.logical_not(live_at(tick, c)))
        def _():
            dst[...] = jnp.zeros(dst.shape, dst.dtype)

    loads[0].wait()
    for d in range(n):
        normalise(0, d, pick(inflow, *lane0[d]))
    loads[1].wait()
    h = forward(0)
    loads[2].wait()
    emit(0, h)
    loads[3].wait()
    for s in range(n):
        ups[2, s] = pick(cot, rank2[s], sent1[s])

    receive(0, True, 1)
    for d in range(n):
        normalise(1, d, pick(landed0, *lane1[d]))
    emit(1, forward(1))

    receive(1, True, 2)
    for s in range(n):
        normalise(2, s, landed1[s])
    forward(2)

    def backward(tick):
        at = pl.ds(tick * tick_rows, tick_rows)
        grad_hidden = dot(ups[tick].reshape(tick_rows, features), we[...], NT)
        p = pre[at, :]
        sig = 1.0 / (1.0 + jnp.exp(-p))
        g = (grad_hidden * sig * (1.0 + p * (1.0 - sig))).astype(jnp.bfloat16)
        gp[at, :] = g
        if tick == 0:
            return
        inner = jnp.sum(g.astype(jnp.float32) * p, axis=-1, keepdims=True) * (1.0 / features)
        scale = inv[at, :][:, :1]
        for start, size in column_chunks:
            cols = pl.ds(start, size)
            grad_unit = dot(g, wr[:, cols], NN)
            unit = lanes[tick, :, :, cols].astype(jnp.float32).reshape(tick_rows, size) * scale
            up = ups[tick, :, :, cols].astype(jnp.float32).reshape(tick_rows, size)
            value = up + scale * (grad_unit - unit * inner)
            value = value.astype(jnp.bfloat16).reshape(n, rows, size)
            if tick == 2:
                bwd_out[1, :, :, cols] = value
            else:
                back[:, :, cols] = value
        if tick == 1:
            for s in range(n):
                bwd_out[0, s] = pick(back, dest1[s], sent0[s])

        @pl.when(live_at(tick, c))
        def _():
            for copy in hop_copies(tick - 1, False):
                copy.start()

    backward(2)
    receive(1, False, 1)
    backward(1)
    receive(0, False, 0)
    backward(0)

    left = [gp[...], hid[...]]
    left = [v.astype(jnp.float32).T.astype(jnp.bfloat16) for v in left]
    for q in range(n):
        cols = pl.ds(q * share, share)
        part[q, 0] = dot(left[0], normed[:, cols], NN).astype(jnp.bfloat16)
        right = ups[:, :, :, cols].reshape(TICKS * tick_rows, share)
        part[q, 1] = dot(left[1], right, NN).astype(jnp.bfloat16)

    def chain(buf, sems, q, m, to):
        return pltpu.make_async_remote_copy(
            src_ref=buf.at[q, m],
            dst_ref=buf.at[q, m],
            send_sem=sems[0].at[q, m],
            recv_sem=sems[1].at[q, m],
            device_id=(c, to),
            device_id_type=MESH,
        )

    flows = [
        (up_buf, (up_send, up_recv), r, 1),
        (down_buf, (down_send, down_recv), n - 1 - r, -1),
    ]
    for slot in range(n - 1):
        for m in range(2):
            for buf, sems, distance, direction in flows:
                late = slot - distance

                @pl.when(late >= 0)
                def _():
                    q = n - 1 - late if direction > 0 else late
                    copy = chain(buf, sems, q, m, r + direction)

                    @pl.when(distance == 0)
                    def _():
                        buf[q, m] = part[q, m]

                    @pl.when(distance > 0)
                    def _():
                        copy.wait_recv()
                        buf[q, m] = (
                            buf[q, m].astype(jnp.float32) + part[q, m].astype(jnp.float32)
                        ).astype(jnp.bfloat16)

                    copy.start()

    for m in range(2):
        @pl.when(r == 0)
        def _():
            chain(down_buf, (down_send, down_recv), r, m, r).wait_recv()
            out[m, 0] = (
                part[r, m].astype(jnp.float32) + down_buf[r, m].astype(jnp.float32)
            ).astype(jnp.bfloat16)

        @pl.when(r == n - 1)
        def _():
            chain(up_buf, (up_send, up_recv), r, m, r).wait_recv()
            out[m, 0] = (
                part[r, m].astype(jnp.float32) + up_buf[r, m].astype(jnp.float32)
            ).astype(jnp.bfloat16)

        @pl.when((r > 0) & (r < n - 1))
        def _():
            chain(down_buf, (down_send, down_recv), r, m, r).wait_recv()
            chain(up_buf, (up_send, up_recv), r, m, r).wait_recv()
            out[m, 0] = (
                part[r, m].astype(jnp.float32)
                + down_buf[r, m].astype(jnp.float32)
                + up_buf[r, m].astype(jnp.float32)
            ).astype(jnp.bfloat16)

    for slot in range(n - 1):
        for m in range(2):
            for buf, sems, distance, direction in flows:
                late = slot - distance

                @pl.when(late >= 0)
                def _():
                    q = n - 1 - late if direction > 0 else late
                    chain(buf, sems, q, m, r + direction).wait_send()
    for hop in range(HOPS):
        @pl.when(live_at(hop, c))
        def _():
            for copy in hop_copies(hop, True):
                copy.wait_send()

        @pl.when(live_at(hop + 1, c))
        def _():
            for copy in hop_copies(hop, False):
                copy.wait_send()


def local(sections, n, inflow, cotangent, reduce_weight, expand_weight, held, routes):
    cap, rows, features = inflow.shape[2:]
    rank = reduce_weight.shape[3]
    share = features // n
    total = TICKS * n * rows
    bf16, f32 = jnp.bfloat16, jnp.float32
    dma = pltpu.SemaphoreType.DMA
    smem = pl.BlockSpec(memory_space=pltpu.SMEM)
    anywhere = pl.BlockSpec(memory_space=pl.ANY)
    lane_set = (n, rows, features)
    grads = pl.pallas_call(
        functools.partial(kernel, sections, n, cap, rows, features, rank),
        out_shape=jax.ShapeDtypeStruct((2, 1, rank, share), bf16),
        in_specs=[smem, smem, anywhere, anywhere, anywhere, anywhere],
        out_specs=pl.BlockSpec(memory_space=pltpu.VMEM),
        scratch_shapes=[
            pltpu.VMEM((cap, rows, features), bf16),
            pltpu.VMEM((cap, rows, features), bf16),
            pltpu.VMEM((rank, features), bf16),
            pltpu.VMEM((rank, features), bf16),
            pltpu.VMEM((TICKS,) + lane_set, bf16),
            pltpu.VMEM(lane_set, bf16),
            pltpu.VMEM(lane_set, bf16),
            pltpu.VMEM((HOPS,) + lane_set, bf16),
            pltpu.VMEM((HOPS,) + lane_set, bf16),
            pltpu.VMEM(lane_set, bf16),
            pltpu.VMEM((TICKS,) + lane_set, bf16),
            pltpu.VMEM((total, features), bf16),
            pltpu.VMEM((total, 128), f32),
            pltpu.VMEM((total, rank), f32),
            pltpu.VMEM((total, rank), bf16),
            pltpu.VMEM((total, rank), bf16),
            pltpu.VMEM((n, 2, rank, share), bf16),
            pltpu.VMEM((n, 2, rank, share), bf16),
            pltpu.VMEM((n, 2, rank, share), bf16),
            dma((4,)),
            dma((HOPS, n)), dma((HOPS, n)), dma((HOPS, n)), dma((HOPS, n)),
            dma((n, 2)), dma((n, 2)), dma((n, 2)), dma((n, 2)),
        ],
        compiler_params=pltpu.CompilerParams(
            collective_id=0, has_side_effects=True, vmem_limit_bytes=56 * 1024 * 1024
        ),
    )(
        held,
        routes,
        inflow[0, 0],
        cotangent[0, 0],
        jnp.swapaxes(reduce_weight[0, 0], 0, 1),
        jnp.swapaxes(expand_weight[0, 0], 0, 1),
    )
    return (jnp.swapaxes(grads[0], 1, 2), jnp.swapaxes(grads[1], 1, 2))


def solution(mesh):
    placed = (
        P("section", "rep", None, None, None),
        P("section", "rep", None, None, None),
        P("section", "rep", None, None),
        P("section", "rep", None, None),
        P(),
        P(),
    )
    return jax.shard_map(
        functools.partial(local, mesh.shape["section"], mesh.shape["rep"]),
        mesh=mesh,
        in_specs=placed,
        out_specs=(P("section", "rep", None), P("section", "rep", None)),
        check_vma=False,
    )
```

```python
import functools

import jax
import jax.numpy as jnp
from jax import lax
from jax.experimental import pallas as pl
from jax.experimental.pallas import tpu as pltpu
from jax.sharding import PartitionSpec as P

TICKS = 3
HOPS = TICKS - 1
HALVES = 2
EPS = 1e-06
MESH = pl.DeviceIdType.MESH
NT = (((1,), (1,)), ((), ()))
NN = (((1,), (0,)), ((), ()))


def dot(a, b, dims):
    return lax.dot_general(a, b, dims, preferred_element_type=jnp.float32)


def chunks(total, size):
    return [(start, min(size, total - start)) for start in range(0, total, size)]


def kernel(
    sections, n, cap, rows, features, rank,
    held, routes, inflow_hbm, cot_hbm, wr_hbm, we_hbm,
    out,
    inflow, cot, wr, we,
    lanes, landed0, landed1, fwd_out, bwd_out, back, ups, normed, inv, pre, hid, gp,
    part, up_buf, down_buf,
    load_sem, send_sem, recv_sem, bsend_sem, brecv_sem,
    up_send, up_recv, down_send, down_recv,
):
    c = lax.axis_index("section")
    r = lax.axis_index("rep")
    tick_rows = n * rows
    share = features // n
    half = features // HALVES
    halves = [
        (pl.ds(h * half, half), [(h * half + a, b) for a, b in chunks(half, 896)])
        for h in range(HALVES)
    ]
    landed = (landed0, landed1)

    loads = [
        pltpu.make_async_copy(src, dst, load_sem.at[i])
        for i, (src, dst) in enumerate(
            [(inflow_hbm, inflow), (wr_hbm, wr), (we_hbm, we), (cot_hbm, cot)]
        )
    ]
    for load in loads:
        load.start()

    barrier = pltpu.get_barrier_semaphore()
    for step in (1, -1):
        other = c + step

        @pl.when((other >= 0) & (other < sections))
        def _():
            for d in range(n):
                pl.semaphore_signal(barrier, inc=1, device_id=(other, d), device_id_type=MESH)

        near = r + step

        @pl.when((near >= 0) & (near < n))
        def _():
            pl.semaphore_signal(barrier, inc=1, device_id=(c, near), device_id_type=MESH)

    def one_if(condition):
        return condition.astype(jnp.int32)

    pl.semaphore_wait(
        barrier,
        n * (one_if(c > 0) + one_if(c < sections - 1)) + one_if(r > 0) + one_if(r < n - 1),
    )

    prev = jnp.maximum(c - 1, 0)
    prev2 = jnp.maximum(c - 2, 0)
    zero = jnp.int32(0)

    def first_tick_sends(section, s, dest):
        def step(k, carry):
            slot, seen = carry
            hit = ((routes[0, section, s, k] == dest) & (k < held[section, s])).astype(jnp.int32)
            return slot + hit * k, seen + hit
        return lax.fori_loop(0, cap, step, (zero, zero), unroll=cap <= 4)

    lane0 = [first_tick_sends(c, r, d) for d in range(n)]
    sent0 = [
        first_tick_sends(prev, s, r)[1] * (c >= 1).astype(jnp.int32) for s in range(n)
    ]

    def ranks(sent):
        total, out_ranks = zero, []
        for s in range(n):
            out_ranks.append(total)
            total = total + sent[s]
        return out_ranks

    rank1 = [jnp.minimum(v, cap - 1) for v in ranks(sent0)]
    dest1 = [routes[1, c, r, rank1[s]] for s in range(n)]
    lane1 = []
    for d in range(n):
        index, seen = zero, zero
        for s in range(n):
            hit = sent0[s] * (dest1[s] == d).astype(jnp.int32)
            index, seen = index + hit * s, seen + hit
        lane1.append((index, seen))

    def count1(s):
        def step(s0, total):
            return total + first_tick_sends(prev2, s0, s)[1]
        return lax.fori_loop(0, n, step, zero, unroll=n <= 4) * (c >= 2).astype(jnp.int32)

    sent1 = []
    for s in range(n):
        count = count1(s)

        def step(k, seen, s=s, count=count):
            return seen + ((routes[1, prev, s, k] == r) & (k < count)).astype(jnp.int32)
        sent1.append(lax.fori_loop(0, cap, step, zero, unroll=cap <= 4))
    rank2 = [jnp.minimum(v, cap - 1) for v in ranks(sent1)]

    def pick(source, index, seen):
        value = source[pl.ds(index, 1)][0]
        return jnp.where(seen > 0, value, jnp.zeros_like(value))

    def live_at(tick, section):
        return (section >= tick) & (section <= sections - TICKS + tick)

    def hop_copies(hop, forward, h):
        buf = fwd_out if forward else bwd_out
        dst = landed[hop] if forward else ups.at[hop]
        sems = (send_sem, recv_sem) if forward else (bsend_sem, brecv_sem)
        target = c + 1 if forward else c - 1
        return [
            pltpu.make_async_remote_copy(
                src_ref=buf.at[hop, d, :, halves[h][0]],
                dst_ref=dst.at[r, :, halves[h][0]],
                send_sem=sems[0].at[hop, d, h],
                recv_sem=sems[1].at[hop, r, h],
                device_id=(target, d),
                device_id_type=MESH,
            )
            for d in range(n)
        ]

    def await_lane(hop, forward, s):
        buf = fwd_out if forward else bwd_out
        dst = landed[hop] if forward else ups.at[hop]
        sems = (send_sem, recv_sem) if forward else (bsend_sem, brecv_sem)
        for h in range(HALVES):
            pltpu.make_async_remote_copy(
                src_ref=buf.at[hop, s, :, halves[h][0]],
                dst_ref=dst.at[s, :, halves[h][0]],
                send_sem=sems[0].at[hop, s, h],
                recv_sem=sems[1].at[hop, s, h],
                device_id=(c, s),
                device_id_type=MESH,
            ).wait_recv()

    def normalise(tick, i, lane):
        lanes[tick, i] = lane
        wide = lane.astype(jnp.float32)
        scale = lax.rsqrt(jnp.mean(wide * wide, axis=-1, keepdims=True) + EPS)
        at = pl.ds(tick * tick_rows + i * rows, rows)
        inv[at, :] = jnp.broadcast_to(scale, (rows, 128))
        normed[at, :] = (wide * scale).astype(jnp.bfloat16)

    def forward(tick):
        at = pl.ds(tick * tick_rows, tick_rows)
        p = dot(normed[at, :], wr[...], NT)
        pre[at, :] = p
        h = (p / (1.0 + jnp.exp(-p))).astype(jnp.bfloat16)
        hid[at, :] = h
        return h

    def emit(tick, hidden):
        for h, (_, parts) in enumerate(halves):
            for start, size in parts:
                cols = pl.ds(start, size)
                branch = dot(hidden, we[:, cols], NN).reshape(n, rows, size)
                fwd_out[tick, :, :, cols] = (
                    lanes[tick, :, :, cols].astype(jnp.float32) + branch
                ).astype(jnp.bfloat16)

            @pl.when(live_at(tick, c))
            def _():
                for copy in hop_copies(tick, True, h):
                    copy.start()

    def receive(hop, forward, tick, s):
        dst = landed[hop] if forward else ups.at[hop]

        @pl.when(live_at(tick, c))
        def _():
            await_lane(hop, forward, s)

        @pl.when(jnp.logical_not(live_at(tick, c)))
        def _():
            dst[s] = jnp.zeros(dst.shape[1:], dst.dtype)

    def receive_all(hop, forward, tick):
        for s in range(n):
            receive(hop, forward, tick, s)

    loads[0].wait()
    for d in range(n):
        normalise(0, d, pick(inflow, *lane0[d]))
    loads[1].wait()
    h = forward(0)
    loads[2].wait()
    emit(0, h)
    loads[3].wait()
    for s in range(n):
        ups[2, s] = pick(cot, rank2[s], sent1[s])

    receive_all(0, True, 1)
    for d in range(n):
        normalise(1, d, pick(landed0, *lane1[d]))
    emit(1, forward(1))

    for s in range(n):
        receive(1, True, 2, s)
        normalise(2, s, landed1[s])
    forward(2)

    def backward(tick):
        at = pl.ds(tick * tick_rows, tick_rows)
        grad_hidden = dot(ups[tick].reshape(tick_rows, features), we[...], NT)
        p = pre[at, :]
        sig = 1.0 / (1.0 + jnp.exp(-p))
        g = (grad_hidden * sig * (1.0 + p * (1.0 - sig))).astype(jnp.bfloat16)
        gp[at, :] = g
        if tick == 0:
            return
        inner = jnp.sum(g.astype(jnp.float32) * p, axis=-1, keepdims=True) * (1.0 / features)
        scale = inv[at, :][:, :1]
        for h, (half_cols, parts) in enumerate(halves):
            for start, size in parts:
                cols = pl.ds(start, size)
                grad_unit = dot(g, wr[:, cols], NN)
                unit = lanes[tick, :, :, cols].astype(jnp.float32).reshape(tick_rows, size) * scale
                up = ups[tick, :, :, cols].astype(jnp.float32).reshape(tick_rows, size)
                value = up + scale * (grad_unit - unit * inner)
                value = value.astype(jnp.bfloat16).reshape(n, rows, size)
                if tick == 2:
                    bwd_out[1, :, :, cols] = value
                else:
                    back[:, :, cols] = value
            if tick == 1:
                for s in range(n):
                    value = back[pl.ds(dest1[s], 1), :, half_cols][0]
                    bwd_out[0, s, :, half_cols] = jnp.where(
                        sent0[s] > 0, value, jnp.zeros_like(value)
                    )

            @pl.when(live_at(tick, c))
            def _():
                for copy in hop_copies(tick - 1, False, h):
                    copy.start()

    backward(2)
    receive_all(1, False, 1)
    backward(1)
    receive_all(0, False, 0)
    backward(0)

    left = [gp[...], hid[...]]
    left = [v.astype(jnp.float32).T.astype(jnp.bfloat16) for v in left]
    def chain(buf, sems, q, m, to, first=False):
        return pltpu.make_async_remote_copy(
            src_ref=(part if first else buf).at[q, m],
            dst_ref=buf.at[q, m],
            send_sem=sems[0].at[q, m],
            recv_sem=sems[1].at[q, m],
            device_id=(c, to),
            device_id_type=MESH,
        )

    flows = [
        (up_buf, (up_send, up_recv), r, 1),
        (down_buf, (down_send, down_recv), n - 1 - r, -1),
    ]

    def make_part(q, m):
        cols = pl.ds(q * share, share)
        if m == 0:
            right = normed[:, cols]
        else:
            right = ups[:, :, :, cols].reshape(TICKS * tick_rows, share)
        part[q, m] = dot(left[m], right, NN).astype(jnp.bfloat16)

    for m in range(2):
        for q, (buf, sems, distance, direction) in zip((n - 1, 0), flows):
            make_part(q, m)

            @pl.when(distance == 0)
            def _():
                chain(buf, sems, q, m, r + direction, True).start()

    for q in range(n - 2, 0, -1):
        for m in range(2):
            make_part(q, m)

    for slot in range(1, n - 1):
        for m in range(2):
            for buf, sems, distance, direction in flows:
                late = slot - distance
                q = n - 1 - late if direction > 0 else late

                @pl.when(distance == 0)
                def _():
                    chain(buf, sems, q, m, r + direction, True).start()

                @pl.when((late >= 0) & (distance > 0))
                def _():
                    copy = chain(buf, sems, q, m, r + direction)
                    copy.wait_recv()
                    buf[q, m] = (
                        buf[q, m].astype(jnp.float32) + part[q, m].astype(jnp.float32)
                    ).astype(jnp.bfloat16)
                    copy.start()

    for m in range(2):
        @pl.when(r == 0)
        def _():
            chain(down_buf, (down_send, down_recv), r, m, r).wait_recv()
            out[m, 0] = (
                part[r, m].astype(jnp.float32) + down_buf[r, m].astype(jnp.float32)
            ).astype(jnp.bfloat16)

        @pl.when(r == n - 1)
        def _():
            chain(up_buf, (up_send, up_recv), r, m, r).wait_recv()
            out[m, 0] = (
                part[r, m].astype(jnp.float32) + up_buf[r, m].astype(jnp.float32)
            ).astype(jnp.bfloat16)

        @pl.when((r > 0) & (r < n - 1))
        def _():
            chain(down_buf, (down_send, down_recv), r, m, r).wait_recv()
            chain(up_buf, (up_send, up_recv), r, m, r).wait_recv()
            out[m, 0] = (
                part[r, m].astype(jnp.float32)
                + down_buf[r, m].astype(jnp.float32)
                + up_buf[r, m].astype(jnp.float32)
            ).astype(jnp.bfloat16)

    for slot in range(n - 1):
        for m in range(2):
            for buf, sems, distance, direction in flows:
                late = slot - distance

                @pl.when(late >= 0)
                def _():
                    q = n - 1 - late if direction > 0 else late
                    chain(buf, sems, q, m, r + direction).wait_send()
    for hop in range(HOPS):
        @pl.when(live_at(hop, c))
        def _():
            for h in range(HALVES):
                for copy in hop_copies(hop, True, h):
                    copy.wait_send()

        @pl.when(live_at(hop + 1, c))
        def _():
            for h in range(HALVES):
                for copy in hop_copies(hop, False, h):
                    copy.wait_send()


def local(sections, n, inflow, cotangent, reduce_weight, expand_weight, held, routes):
    cap, rows, features = inflow.shape[2:]
    rank = reduce_weight.shape[3]
    share = features // n
    total = TICKS * n * rows
    bf16, f32 = jnp.bfloat16, jnp.float32
    dma = pltpu.SemaphoreType.DMA
    smem = pl.BlockSpec(memory_space=pltpu.SMEM)
    anywhere = pl.BlockSpec(memory_space=pl.ANY)
    lane_set = (n, rows, features)
    grads = pl.pallas_call(
        functools.partial(kernel, sections, n, cap, rows, features, rank),
        out_shape=jax.ShapeDtypeStruct((2, 1, rank, share), bf16),
        in_specs=[smem, smem, anywhere, anywhere, anywhere, anywhere],
        out_specs=pl.BlockSpec(memory_space=pltpu.VMEM),
        scratch_shapes=[
            pltpu.VMEM((cap, rows, features), bf16),
            pltpu.VMEM((cap, rows, features), bf16),
            pltpu.VMEM((rank, features), bf16),
            pltpu.VMEM((rank, features), bf16),
            pltpu.VMEM((TICKS,) + lane_set, bf16),
            pltpu.VMEM(lane_set, bf16),
            pltpu.VMEM(lane_set, bf16),
            pltpu.VMEM((HOPS,) + lane_set, bf16),
            pltpu.VMEM((HOPS,) + lane_set, bf16),
            pltpu.VMEM(lane_set, bf16),
            pltpu.VMEM((TICKS,) + lane_set, bf16),
            pltpu.VMEM((total, features), bf16),
            pltpu.VMEM((total, 128), f32),
            pltpu.VMEM((total, rank), f32),
            pltpu.VMEM((total, rank), bf16),
            pltpu.VMEM((total, rank), bf16),
            pltpu.VMEM((n, 2, rank, share), bf16),
            pltpu.VMEM((n, 2, rank, share), bf16),
            pltpu.VMEM((n, 2, rank, share), bf16),
            dma((4,)),
            dma((HOPS, n, HALVES)), dma((HOPS, n, HALVES)), dma((HOPS, n, HALVES)), dma((HOPS, n, HALVES)),
            dma((n, 2)), dma((n, 2)), dma((n, 2)), dma((n, 2)),
        ],
        compiler_params=pltpu.CompilerParams(
            collective_id=0, has_side_effects=True, vmem_limit_bytes=56 * 1024 * 1024
        ),
    )(
        held,
        routes,
        inflow[0, 0],
        cotangent[0, 0],
        jnp.swapaxes(reduce_weight[0, 0], 0, 1),
        jnp.swapaxes(expand_weight[0, 0], 0, 1),
    )
    return (jnp.swapaxes(grads[0], 1, 2), jnp.swapaxes(grads[1], 1, 2))


def solution(mesh):
    placed = (
        P("section", "rep", None, None, None),
        P("section", "rep", None, None, None),
        P("section", "rep", None, None),
        P("section", "rep", None, None),
        P(),
        P(),
    )
    return jax.shard_map(
        functools.partial(local, mesh.shape["section"], mesh.shape["rep"]),
        mesh=mesh,
        in_specs=placed,
        out_specs=(P("section", "rep", None), P("section", "rep", None)),
        check_vma=False,
    )
```

```python
import functools

import jax
import jax.numpy as jnp
from jax import lax
from jax.experimental import pallas as pl
from jax.experimental.pallas import tpu as pltpu
from jax.sharding import PartitionSpec as P

TICKS = 3
HOPS = TICKS - 1
HALVES = 2
EPS = 1e-06
MESH = pl.DeviceIdType.MESH
NT = (((1,), (1,)), ((), ()))
NN = (((1,), (0,)), ((), ()))


def dot(a, b, dims):
    return lax.dot_general(a, b, dims, preferred_element_type=jnp.float32)


def chunks(total, size):
    return [(start, min(size, total - start)) for start in range(0, total, size)]


def kernel(
    sections, n, cap, rows, features, rank,
    held, routes, inflow_hbm, cot_hbm, wr_hbm, we_hbm,
    out,
    inflow, cot, wr, we,
    lanes, landed0, landed1, fwd_out, bwd_out, back, ups, normed, inv, pre, hid, gp,
    part, up_buf, down_buf,
    load_sem, send_sem, recv_sem, bsend_sem, brecv_sem,
    up_send, up_recv, down_send, down_recv,
):
    c = lax.axis_index("section")
    r = lax.axis_index("rep")
    tick_rows = n * rows
    share = features // n
    half = features // HALVES
    halves = [
        (pl.ds(h * half, half), [(h * half + a, b) for a, b in chunks(half, 896)])
        for h in range(HALVES)
    ]
    landed = (landed0, landed1)

    loads = [
        pltpu.make_async_copy(src, dst, load_sem.at[i])
        for i, (src, dst) in enumerate(
            [(inflow_hbm, inflow), (wr_hbm, wr), (we_hbm, we), (cot_hbm, cot)]
        )
    ]
    for load in loads:
        load.start()

    barrier = pltpu.get_barrier_semaphore()
    for step in (1, -1):
        other = c + step

        @pl.when((other >= 0) & (other < sections))
        def _():
            for d in range(n):
                pl.semaphore_signal(barrier, inc=1, device_id=(other, d), device_id_type=MESH)

        near = r + step

        @pl.when((near >= 0) & (near < n))
        def _():
            pl.semaphore_signal(barrier, inc=1, device_id=(c, near), device_id_type=MESH)

    def one_if(condition):
        return condition.astype(jnp.int32)

    pl.semaphore_wait(
        barrier,
        n * (one_if(c > 0) + one_if(c < sections - 1)) + one_if(r > 0) + one_if(r < n - 1),
    )

    prev = jnp.maximum(c - 1, 0)
    prev2 = jnp.maximum(c - 2, 0)
    zero = jnp.int32(0)

    def first_tick_sends(section, s, dest):
        def step(k, carry):
            slot, seen = carry
            hit = ((routes[0, section, s, k] == dest) & (k < held[section, s])).astype(jnp.int32)
            return slot + hit * k, seen + hit
        return lax.fori_loop(0, cap, step, (zero, zero), unroll=cap <= 4)

    lane0 = [first_tick_sends(c, r, d) for d in range(n)]
    sent0 = [
        first_tick_sends(prev, s, r)[1] * (c >= 1).astype(jnp.int32) for s in range(n)
    ]

    def ranks(sent):
        total, out_ranks = zero, []
        for s in range(n):
            out_ranks.append(total)
            total = total + sent[s]
        return out_ranks

    rank1 = [jnp.minimum(v, cap - 1) for v in ranks(sent0)]
    dest1 = [routes[1, c, r, rank1[s]] for s in range(n)]
    lane1 = []
    for d in range(n):
        index, seen = zero, zero
        for s in range(n):
            hit = sent0[s] * (dest1[s] == d).astype(jnp.int32)
            index, seen = index + hit * s, seen + hit
        lane1.append((index, seen))

    def count1(s):
        def step(s0, total):
            return total + first_tick_sends(prev2, s0, s)[1]
        return lax.fori_loop(0, n, step, zero, unroll=n <= 4) * (c >= 2).astype(jnp.int32)

    sent1 = []
    for s in range(n):
        count = count1(s)

        def step(k, seen, s=s, count=count):
            return seen + ((routes[1, prev, s, k] == r) & (k < count)).astype(jnp.int32)
        sent1.append(lax.fori_loop(0, cap, step, zero, unroll=cap <= 4))
    rank2 = [jnp.minimum(v, cap - 1) for v in ranks(sent1)]

    def pick(source, index, seen):
        value = source[pl.ds(index, 1)][0]
        return jnp.where(seen > 0, value, jnp.zeros_like(value))

    order = [lax.rem(r + (n // 2 + j) % n, n) for j in range(n) if (n // 2 + j) % n] + [r]

    def live_at(tick, section):
        return (section >= tick) & (section <= sections - TICKS + tick)

    def hop_copies(hop, forward, h):
        buf = fwd_out if forward else bwd_out
        dst = landed[hop] if forward else ups.at[hop]
        sems = (send_sem, recv_sem) if forward else (bsend_sem, brecv_sem)
        target = c + 1 if forward else c - 1
        return [
            pltpu.make_async_remote_copy(
                src_ref=buf.at[hop, d, :, halves[h][0]],
                dst_ref=dst.at[r, :, halves[h][0]],
                send_sem=sems[0].at[hop, d, h],
                recv_sem=sems[1].at[hop, r, h],
                device_id=(target, d),
                device_id_type=MESH,
            )
            for d in order
        ]

    def await_lane(hop, forward, s):
        buf = fwd_out if forward else bwd_out
        dst = landed[hop] if forward else ups.at[hop]
        sems = (send_sem, recv_sem) if forward else (bsend_sem, brecv_sem)
        for h in range(HALVES):
            pltpu.make_async_remote_copy(
                src_ref=buf.at[hop, s, :, halves[h][0]],
                dst_ref=dst.at[s, :, halves[h][0]],
                send_sem=sems[0].at[hop, s, h],
                recv_sem=sems[1].at[hop, s, h],
                device_id=(c, s),
                device_id_type=MESH,
            ).wait_recv()

    def normalise(tick, i, lane):
        lanes[tick, i] = lane
        wide = lane.astype(jnp.float32)
        scale = lax.rsqrt(jnp.mean(wide * wide, axis=-1, keepdims=True) + EPS)
        at = pl.ds(tick * tick_rows + i * rows, rows)
        inv[at, :] = jnp.broadcast_to(scale, (rows, 128))
        normed[at, :] = (wide * scale).astype(jnp.bfloat16)

    def forward(tick):
        at = pl.ds(tick * tick_rows, tick_rows)
        p = dot(normed[at, :], wr[...], NT)
        pre[at, :] = p
        h = (p / (1.0 + jnp.exp(-p))).astype(jnp.bfloat16)
        hid[at, :] = h
        return h

    def emit(tick, hidden):
        for h, (_, parts) in enumerate(halves):
            for start, size in parts:
                cols = pl.ds(start, size)
                branch = dot(hidden, we[:, cols], NN).reshape(n, rows, size)
                fwd_out[tick, :, :, cols] = (
                    lanes[tick, :, :, cols].astype(jnp.float32) + branch
                ).astype(jnp.bfloat16)

            @pl.when(live_at(tick, c))
            def _():
                for copy in hop_copies(tick, True, h):
                    copy.start()

    def receive(hop, forward, tick, s):
        dst = landed[hop] if forward else ups.at[hop]

        @pl.when(live_at(tick, c))
        def _():
            await_lane(hop, forward, s)

        @pl.when(jnp.logical_not(live_at(tick, c)))
        def _():
            dst[s] = jnp.zeros(dst.shape[1:], dst.dtype)

    def receive_all(hop, forward, tick):
        for s in range(n):
            receive(hop, forward, tick, s)

    loads[0].wait()
    for d in range(n):
        normalise(0, d, pick(inflow, *lane0[d]))
    loads[1].wait()
    h = forward(0)
    loads[2].wait()
    emit(0, h)
    loads[3].wait()
    for s in range(n):
        ups[2, s] = pick(cot, rank2[s], sent1[s])

    receive_all(0, True, 1)
    for d in range(n):
        normalise(1, d, pick(landed0, *lane1[d]))
    emit(1, forward(1))

    for s in range(n):
        receive(1, True, 2, s)
        normalise(2, s, landed1[s])
    forward(2)

    def backward(tick):
        at = pl.ds(tick * tick_rows, tick_rows)
        grad_hidden = dot(ups[tick].reshape(tick_rows, features), we[...], NT)
        p = pre[at, :]
        sig = 1.0 / (1.0 + jnp.exp(-p))
        g = (grad_hidden * sig * (1.0 + p * (1.0 - sig))).astype(jnp.bfloat16)
        gp[at, :] = g
        if tick == 0:
            return
        inner = jnp.sum(g.astype(jnp.float32) * p, axis=-1, keepdims=True) * (1.0 / features)
        scale = inv[at, :][:, :1]
        for h, (half_cols, parts) in enumerate(halves):
            for start, size in parts:
                cols = pl.ds(start, size)
                grad_unit = dot(g, wr[:, cols], NN)
                unit = lanes[tick, :, :, cols].astype(jnp.float32).reshape(tick_rows, size) * scale
                up = ups[tick, :, :, cols].astype(jnp.float32).reshape(tick_rows, size)
                value = up + scale * (grad_unit - unit * inner)
                value = value.astype(jnp.bfloat16).reshape(n, rows, size)
                if tick == 2:
                    bwd_out[1, :, :, cols] = value
                else:
                    back[:, :, cols] = value
            if tick == 1:
                for s in range(n):
                    value = back[pl.ds(dest1[s], 1), :, half_cols][0]
                    bwd_out[0, s, :, half_cols] = jnp.where(
                        sent0[s] > 0, value, jnp.zeros_like(value)
                    )

            @pl.when(live_at(tick, c))
            def _():
                for copy in hop_copies(tick - 1, False, h):
                    copy.start()

    backward(2)
    receive_all(1, False, 1)
    backward(1)
    receive_all(0, False, 0)
    backward(0)

    left = [gp[...], hid[...]]
    left = [v.astype(jnp.float32).T.astype(jnp.bfloat16) for v in left]
    def chain(buf, sems, q, m, to, first=False):
        return pltpu.make_async_remote_copy(
            src_ref=(part if first else buf).at[q, m],
            dst_ref=buf.at[q, m],
            send_sem=sems[0].at[q, m],
            recv_sem=sems[1].at[q, m],
            device_id=(c, to),
            device_id_type=MESH,
        )

    flows = [
        (up_buf, (up_send, up_recv), r, 1),
        (down_buf, (down_send, down_recv), n - 1 - r, -1),
    ]

    def make_part(q, m):
        cols = pl.ds(q * share, share)
        if m == 0:
            right = normed[:, cols]
        else:
            right = ups[:, :, :, cols].reshape(TICKS * tick_rows, share)
        part[q, m] = dot(left[m], right, NN).astype(jnp.bfloat16)

    for m in range(2):
        for q, (buf, sems, distance, direction) in zip((n - 1, 0), flows):
            make_part(q, m)

            @pl.when(distance == 0)
            def _():
                chain(buf, sems, q, m, r + direction, True).start()

    for q in range(n - 2, 0, -1):
        for m in range(2):
            make_part(q, m)

    for slot in range(1, n - 1):
        for m in range(2):
            for buf, sems, distance, direction in flows:
                late = slot - distance
                q = n - 1 - late if direction > 0 else late

                @pl.when(distance == 0)
                def _():
                    chain(buf, sems, q, m, r + direction, True).start()

                @pl.when((late >= 0) & (distance > 0))
                def _():
                    copy = chain(buf, sems, q, m, r + direction)
                    copy.wait_recv()
                    buf[q, m] = (
                        buf[q, m].astype(jnp.float32) + part[q, m].astype(jnp.float32)
                    ).astype(jnp.bfloat16)
                    copy.start()

    for m in range(2):
        @pl.when(r == 0)
        def _():
            chain(down_buf, (down_send, down_recv), r, m, r).wait_recv()
            out[m, 0] = (
                part[r, m].astype(jnp.float32) + down_buf[r, m].astype(jnp.float32)
            ).astype(jnp.bfloat16)

        @pl.when(r == n - 1)
        def _():
            chain(up_buf, (up_send, up_recv), r, m, r).wait_recv()
            out[m, 0] = (
                part[r, m].astype(jnp.float32) + up_buf[r, m].astype(jnp.float32)
            ).astype(jnp.bfloat16)

        @pl.when((r > 0) & (r < n - 1))
        def _():
            chain(down_buf, (down_send, down_recv), r, m, r).wait_recv()
            chain(up_buf, (up_send, up_recv), r, m, r).wait_recv()
            out[m, 0] = (
                part[r, m].astype(jnp.float32)
                + down_buf[r, m].astype(jnp.float32)
                + up_buf[r, m].astype(jnp.float32)
            ).astype(jnp.bfloat16)

    for slot in range(n - 1):
        for m in range(2):
            for buf, sems, distance, direction in flows:
                late = slot - distance

                @pl.when(late >= 0)
                def _():
                    q = n - 1 - late if direction > 0 else late
                    chain(buf, sems, q, m, r + direction).wait_send()
    for hop in range(HOPS):
        @pl.when(live_at(hop, c))
        def _():
            for h in range(HALVES):
                for copy in hop_copies(hop, True, h):
                    copy.wait_send()

        @pl.when(live_at(hop + 1, c))
        def _():
            for h in range(HALVES):
                for copy in hop_copies(hop, False, h):
                    copy.wait_send()


def local(sections, n, inflow, cotangent, reduce_weight, expand_weight, held, routes):
    cap, rows, features = inflow.shape[2:]
    rank = reduce_weight.shape[3]
    share = features // n
    total = TICKS * n * rows
    bf16, f32 = jnp.bfloat16, jnp.float32
    dma = pltpu.SemaphoreType.DMA
    smem = pl.BlockSpec(memory_space=pltpu.SMEM)
    anywhere = pl.BlockSpec(memory_space=pl.ANY)
    lane_set = (n, rows, features)
    grads = pl.pallas_call(
        functools.partial(kernel, sections, n, cap, rows, features, rank),
        out_shape=jax.ShapeDtypeStruct((2, 1, rank, share), bf16),
        in_specs=[smem, smem, anywhere, anywhere, anywhere, anywhere],
        out_specs=pl.BlockSpec(memory_space=pltpu.VMEM),
        scratch_shapes=[
            pltpu.VMEM((cap, rows, features), bf16),
            pltpu.VMEM((cap, rows, features), bf16),
            pltpu.VMEM((rank, features), bf16),
            pltpu.VMEM((rank, features), bf16),
            pltpu.VMEM((TICKS,) + lane_set, bf16),
            pltpu.VMEM(lane_set, bf16),
            pltpu.VMEM(lane_set, bf16),
            pltpu.VMEM((HOPS,) + lane_set, bf16),
            pltpu.VMEM((HOPS,) + lane_set, bf16),
            pltpu.VMEM(lane_set, bf16),
            pltpu.VMEM((TICKS,) + lane_set, bf16),
            pltpu.VMEM((total, features), bf16),
            pltpu.VMEM((total, 128), f32),
            pltpu.VMEM((total, rank), f32),
            pltpu.VMEM((total, rank), bf16),
            pltpu.VMEM((total, rank), bf16),
            pltpu.VMEM((n, 2, rank, share), bf16),
            pltpu.VMEM((n, 2, rank, share), bf16),
            pltpu.VMEM((n, 2, rank, share), bf16),
            dma((4,)),
            dma((HOPS, n, HALVES)), dma((HOPS, n, HALVES)), dma((HOPS, n, HALVES)), dma((HOPS, n, HALVES)),
            dma((n, 2)), dma((n, 2)), dma((n, 2)), dma((n, 2)),
        ],
        compiler_params=pltpu.CompilerParams(
            collective_id=0, has_side_effects=True, vmem_limit_bytes=56 * 1024 * 1024
        ),
    )(
        held,
        routes,
        inflow[0, 0],
        cotangent[0, 0],
        jnp.swapaxes(reduce_weight[0, 0], 0, 1),
        jnp.swapaxes(expand_weight[0, 0], 0, 1),
    )
    return (jnp.swapaxes(grads[0], 1, 2), jnp.swapaxes(grads[1], 1, 2))


def solution(mesh):
    placed = (
        P("section", "rep", None, None, None),
        P("section", "rep", None, None, None),
        P("section", "rep", None, None),
        P("section", "rep", None, None),
        P(),
        P(),
    )
    return jax.shard_map(
        functools.partial(local, mesh.shape["section"], mesh.shape["rep"]),
        mesh=mesh,
        in_specs=placed,
        out_specs=(P("section", "rep", None), P("section", "rep", None)),
        check_vma=False,
    )
```

```python
import functools

import jax
import jax.numpy as jnp
from jax import lax
from jax.experimental import pallas as pl
from jax.experimental.pallas import tpu as pltpu
from jax.sharding import PartitionSpec as P

TICKS = 3
HOPS = TICKS - 1
HALVES = 1
EPS = 1e-06
MESH = pl.DeviceIdType.MESH
NT = (((1,), (1,)), ((), ()))
NN = (((1,), (0,)), ((), ()))


def dot(a, b, dims):
    return lax.dot_general(a, b, dims, preferred_element_type=jnp.float32)


def chunks(total, size):
    return [(start, min(size, total - start)) for start in range(0, total, size)]


def kernel(
    sections, n, cap, rows, features, rank,
    held, routes, inflow_hbm, cot_hbm, wr_hbm, we_hbm,
    out,
    inflow, cot, wr, we,
    lanes, landed0, landed1, fwd_out, bwd_out, back, ups, normed, inv, pre, hid, gp,
    part, up_buf, down_buf,
    load_sem, send_sem, recv_sem, bsend_sem, brecv_sem,
    up_send, up_recv, down_send, down_recv,
):
    c = lax.axis_index("section")
    r = lax.axis_index("rep")
    tick_rows = n * rows
    share = features // n
    half = features // HALVES
    halves = [
        (pl.ds(h * half, half), [(h * half + a, b) for a, b in chunks(half, 896)])
        for h in range(HALVES)
    ]
    landed = (landed0, landed1)

    loads = [
        pltpu.make_async_copy(src, dst, load_sem.at[i])
        for i, (src, dst) in enumerate(
            [(inflow_hbm, inflow), (wr_hbm, wr), (we_hbm, we), (cot_hbm, cot)]
        )
    ]
    for load in loads:
        load.start()

    barrier = pltpu.get_barrier_semaphore()
    for step in (1, -1):
        other = c + step

        @pl.when((other >= 0) & (other < sections))
        def _():
            for d in range(n):
                pl.semaphore_signal(barrier, inc=1, device_id=(other, d), device_id_type=MESH)

        near = r + step

        @pl.when((near >= 0) & (near < n))
        def _():
            pl.semaphore_signal(barrier, inc=1, device_id=(c, near), device_id_type=MESH)

    def one_if(condition):
        return condition.astype(jnp.int32)

    pl.semaphore_wait(
        barrier,
        n * (one_if(c > 0) + one_if(c < sections - 1)) + one_if(r > 0) + one_if(r < n - 1),
    )

    prev = jnp.maximum(c - 1, 0)
    prev2 = jnp.maximum(c - 2, 0)
    zero = jnp.int32(0)

    def first_tick_sends(section, s, dest):
        def step(k, carry):
            slot, seen = carry
            hit = ((routes[0, section, s, k] == dest) & (k < held[section, s])).astype(jnp.int32)
            return slot + hit * k, seen + hit
        return lax.fori_loop(0, cap, step, (zero, zero), unroll=cap <= 4)

    lane0 = [first_tick_sends(c, r, d) for d in range(n)]
    sent0 = [
        first_tick_sends(prev, s, r)[1] * (c >= 1).astype(jnp.int32) for s in range(n)
    ]

    def ranks(sent):
        total, out_ranks = zero, []
        for s in range(n):
            out_ranks.append(total)
            total = total + sent[s]
        return out_ranks

    rank1 = [jnp.minimum(v, cap - 1) for v in ranks(sent0)]
    dest1 = [routes[1, c, r, rank1[s]] for s in range(n)]
    lane1 = []
    for d in range(n):
        index, seen = zero, zero
        for s in range(n):
            hit = sent0[s] * (dest1[s] == d).astype(jnp.int32)
            index, seen = index + hit * s, seen + hit
        lane1.append((index, seen))

    def count1(s):
        def step(s0, total):
            return total + first_tick_sends(prev2, s0, s)[1]
        return lax.fori_loop(0, n, step, zero, unroll=n <= 4) * (c >= 2).astype(jnp.int32)

    sent1 = []
    for s in range(n):
        count = count1(s)

        def step(k, seen, s=s, count=count):
            return seen + ((routes[1, prev, s, k] == r) & (k < count)).astype(jnp.int32)
        sent1.append(lax.fori_loop(0, cap, step, zero, unroll=cap <= 4))
    rank2 = [jnp.minimum(v, cap - 1) for v in ranks(sent1)]

    def pick(source, index, seen):
        value = source[pl.ds(index, 1)][0]
        return jnp.where(seen > 0, value, jnp.zeros_like(value))

    order = [lax.rem(r + (n // 2 + j) % n, n) for j in range(n) if (n // 2 + j) % n] + [r]

    def live_at(tick, section):
        return (section >= tick) & (section <= sections - TICKS + tick)

    def hop_copies(hop, forward, h):
        buf = fwd_out if forward else bwd_out
        dst = landed[hop] if forward else ups.at[hop]
        sems = (send_sem, recv_sem) if forward else (bsend_sem, brecv_sem)
        target = c + 1 if forward else c - 1
        return [
            pltpu.make_async_remote_copy(
                src_ref=buf.at[hop, d, :, halves[h][0]],
                dst_ref=dst.at[r, :, halves[h][0]],
                send_sem=sems[0].at[hop, d, h],
                recv_sem=sems[1].at[hop, r, h],
                device_id=(target, d),
                device_id_type=MESH,
            )
            for d in order
        ]

    def await_lane(hop, forward, s):
        buf = fwd_out if forward else bwd_out
        dst = landed[hop] if forward else ups.at[hop]
        sems = (send_sem, recv_sem) if forward else (bsend_sem, brecv_sem)
        for h in range(HALVES):
            pltpu.make_async_remote_copy(
                src_ref=buf.at[hop, s, :, halves[h][0]],
                dst_ref=dst.at[s, :, halves[h][0]],
                send_sem=sems[0].at[hop, s, h],
                recv_sem=sems[1].at[hop, s, h],
                device_id=(c, s),
                device_id_type=MESH,
            ).wait_recv()

    def normalise(tick, i, lane):
        lanes[tick, i] = lane
        wide = lane.astype(jnp.float32)
        scale = lax.rsqrt(jnp.mean(wide * wide, axis=-1, keepdims=True) + EPS)
        at = pl.ds(tick * tick_rows + i * rows, rows)
        inv[at, :] = jnp.broadcast_to(scale, (rows, 128))
        normed[at, :] = (wide * scale).astype(jnp.bfloat16)

    def forward(tick):
        at = pl.ds(tick * tick_rows, tick_rows)
        p = dot(normed[at, :], wr[...], NT)
        pre[at, :] = p
        h = (p / (1.0 + jnp.exp(-p))).astype(jnp.bfloat16)
        hid[at, :] = h
        return h

    def emit(tick, hidden):
        for h, (_, parts) in enumerate(halves):
            for start, size in parts:
                cols = pl.ds(start, size)
                branch = dot(hidden, we[:, cols], NN).reshape(n, rows, size)
                fwd_out[tick, :, :, cols] = (
                    lanes[tick, :, :, cols].astype(jnp.float32) + branch
                ).astype(jnp.bfloat16)

            @pl.when(live_at(tick, c))
            def _():
                for copy in hop_copies(tick, True, h):
                    copy.start()

    def receive(hop, forward, tick, s):
        dst = landed[hop] if forward else ups.at[hop]

        @pl.when(live_at(tick, c))
        def _():
            await_lane(hop, forward, s)

        @pl.when(jnp.logical_not(live_at(tick, c)))
        def _():
            dst[s] = jnp.zeros(dst.shape[1:], dst.dtype)

    def receive_all(hop, forward, tick):
        for s in range(n):
            receive(hop, forward, tick, s)

    loads[0].wait()
    for d in range(n):
        normalise(0, d, pick(inflow, *lane0[d]))
    loads[1].wait()
    h = forward(0)
    loads[2].wait()
    emit(0, h)
    loads[3].wait()
    for s in range(n):
        ups[2, s] = pick(cot, rank2[s], sent1[s])

    receive_all(0, True, 1)
    for d in range(n):
        normalise(1, d, pick(landed0, *lane1[d]))
    emit(1, forward(1))

    for s in range(n):
        receive(1, True, 2, s)
        normalise(2, s, landed1[s])
    forward(2)

    def backward(tick):
        at = pl.ds(tick * tick_rows, tick_rows)
        grad_hidden = dot(ups[tick].reshape(tick_rows, features), we[...], NT)
        p = pre[at, :]
        sig = 1.0 / (1.0 + jnp.exp(-p))
        g = (grad_hidden * sig * (1.0 + p * (1.0 - sig))).astype(jnp.bfloat16)
        gp[at, :] = g
        if tick == 0:
            return
        inner = jnp.sum(g.astype(jnp.float32) * p, axis=-1, keepdims=True) * (1.0 / features)
        scale = inv[at, :][:, :1]
        for h, (half_cols, parts) in enumerate(halves):
            for start, size in parts:
                cols = pl.ds(start, size)
                grad_unit = dot(g, wr[:, cols], NN)
                unit = lanes[tick, :, :, cols].astype(jnp.float32).reshape(tick_rows, size) * scale
                up = ups[tick, :, :, cols].astype(jnp.float32).reshape(tick_rows, size)
                value = up + scale * (grad_unit - unit * inner)
                value = value.astype(jnp.bfloat16).reshape(n, rows, size)
                if tick == 2:
                    bwd_out[1, :, :, cols] = value
                else:
                    back[:, :, cols] = value
            if tick == 1:
                for s in range(n):
                    value = back[pl.ds(dest1[s], 1), :, half_cols][0]
                    bwd_out[0, s, :, half_cols] = jnp.where(
                        sent0[s] > 0, value, jnp.zeros_like(value)
                    )

            @pl.when(live_at(tick, c))
            def _():
                for copy in hop_copies(tick - 1, False, h):
                    copy.start()

    backward(2)
    receive_all(1, False, 1)
    backward(1)
    receive_all(0, False, 0)
    backward(0)

    left = [gp[...], hid[...]]
    left = [v.astype(jnp.float32).T.astype(jnp.bfloat16) for v in left]
    def chain(buf, sems, q, m, to, first=False):
        return pltpu.make_async_remote_copy(
            src_ref=(part if first else buf).at[q, m],
            dst_ref=buf.at[q, m],
            send_sem=sems[0].at[q, m],
            recv_sem=sems[1].at[q, m],
            device_id=(c, to),
            device_id_type=MESH,
        )

    flows = [
        (up_buf, (up_send, up_recv), r, 1),
        (down_buf, (down_send, down_recv), n - 1 - r, -1),
    ]

    def make_part(q, m):
        cols = pl.ds(q * share, share)
        if m == 0:
            right = normed[:, cols]
        else:
            right = ups[:, :, :, cols].reshape(TICKS * tick_rows, share)
        part[q, m] = dot(left[m], right, NN).astype(jnp.bfloat16)

    for m in range(2):
        for q, (buf, sems, distance, direction) in zip((n - 1, 0), flows):
            make_part(q, m)

            @pl.when(distance == 0)
            def _():
                chain(buf, sems, q, m, r + direction, True).start()

    for q in range(n - 2, 0, -1):
        for m in range(2):
            make_part(q, m)

    for slot in range(1, n - 1):
        for m in range(2):
            for buf, sems, distance, direction in flows:
                late = slot - distance
                q = n - 1 - late if direction > 0 else late

                @pl.when(distance == 0)
                def _():
                    chain(buf, sems, q, m, r + direction, True).start()

                @pl.when((late >= 0) & (distance > 0))
                def _():
                    copy = chain(buf, sems, q, m, r + direction)
                    copy.wait_recv()
                    buf[q, m] = (
                        buf[q, m].astype(jnp.float32) + part[q, m].astype(jnp.float32)
                    ).astype(jnp.bfloat16)
                    copy.start()

    for m in range(2):
        @pl.when(r == 0)
        def _():
            chain(down_buf, (down_send, down_recv), r, m, r).wait_recv()
            out[m, 0] = (
                part[r, m].astype(jnp.float32) + down_buf[r, m].astype(jnp.float32)
            ).astype(jnp.bfloat16)

        @pl.when(r == n - 1)
        def _():
            chain(up_buf, (up_send, up_recv), r, m, r).wait_recv()
            out[m, 0] = (
                part[r, m].astype(jnp.float32) + up_buf[r, m].astype(jnp.float32)
            ).astype(jnp.bfloat16)

        @pl.when((r > 0) & (r < n - 1))
        def _():
            chain(down_buf, (down_send, down_recv), r, m, r).wait_recv()
            chain(up_buf, (up_send, up_recv), r, m, r).wait_recv()
            out[m, 0] = (
                part[r, m].astype(jnp.float32)
                + down_buf[r, m].astype(jnp.float32)
                + up_buf[r, m].astype(jnp.float32)
            ).astype(jnp.bfloat16)

    for slot in range(n - 1):
        for m in range(2):
            for buf, sems, distance, direction in flows:
                late = slot - distance

                @pl.when(late >= 0)
                def _():
                    q = n - 1 - late if direction > 0 else late
                    chain(buf, sems, q, m, r + direction).wait_send()
    for hop in range(HOPS):
        @pl.when(live_at(hop, c))
        def _():
            for h in range(HALVES):
                for copy in hop_copies(hop, True, h):
                    copy.wait_send()

        @pl.when(live_at(hop + 1, c))
        def _():
            for h in range(HALVES):
                for copy in hop_copies(hop, False, h):
                    copy.wait_send()


def local(sections, n, inflow, cotangent, reduce_weight, expand_weight, held, routes):
    cap, rows, features = inflow.shape[2:]
    rank = reduce_weight.shape[3]
    share = features // n
    total = TICKS * n * rows
    bf16, f32 = jnp.bfloat16, jnp.float32
    dma = pltpu.SemaphoreType.DMA
    smem = pl.BlockSpec(memory_space=pltpu.SMEM)
    anywhere = pl.BlockSpec(memory_space=pl.ANY)
    lane_set = (n, rows, features)
    grads = pl.pallas_call(
        functools.partial(kernel, sections, n, cap, rows, features, rank),
        out_shape=jax.ShapeDtypeStruct((2, 1, rank, share), bf16),
        in_specs=[smem, smem, anywhere, anywhere, anywhere, anywhere],
        out_specs=pl.BlockSpec(memory_space=pltpu.VMEM),
        scratch_shapes=[
            pltpu.VMEM((cap, rows, features), bf16),
            pltpu.VMEM((cap, rows, features), bf16),
            pltpu.VMEM((rank, features), bf16),
            pltpu.VMEM((rank, features), bf16),
            pltpu.VMEM((TICKS,) + lane_set, bf16),
            pltpu.VMEM(lane_set, bf16),
            pltpu.VMEM(lane_set, bf16),
            pltpu.VMEM((HOPS,) + lane_set, bf16),
            pltpu.VMEM((HOPS,) + lane_set, bf16),
            pltpu.VMEM(lane_set, bf16),
            pltpu.VMEM((TICKS,) + lane_set, bf16),
            pltpu.VMEM((total, features), bf16),
            pltpu.VMEM((total, 128), f32),
            pltpu.VMEM((total, rank), f32),
            pltpu.VMEM((total, rank), bf16),
            pltpu.VMEM((total, rank), bf16),
            pltpu.VMEM((n, 2, rank, share), bf16),
            pltpu.VMEM((n, 2, rank, share), bf16),
            pltpu.VMEM((n, 2, rank, share), bf16),
            dma((4,)),
            dma((HOPS, n, HALVES)), dma((HOPS, n, HALVES)), dma((HOPS, n, HALVES)), dma((HOPS, n, HALVES)),
            dma((n, 2)), dma((n, 2)), dma((n, 2)), dma((n, 2)),
        ],
        compiler_params=pltpu.CompilerParams(
            collective_id=0, has_side_effects=True, vmem_limit_bytes=56 * 1024 * 1024
        ),
    )(
        held,
        routes,
        inflow[0, 0],
        cotangent[0, 0],
        jnp.swapaxes(reduce_weight[0, 0], 0, 1),
        jnp.swapaxes(expand_weight[0, 0], 0, 1),
    )
    return (jnp.swapaxes(grads[0], 1, 2), jnp.swapaxes(grads[1], 1, 2))


def solution(mesh):
    placed = (
        P("section", "rep", None, None, None),
        P("section", "rep", None, None, None),
        P("section", "rep", None, None),
        P("section", "rep", None, None),
        P(),
        P(),
    )
    return jax.shard_map(
        functools.partial(local, mesh.shape["section"], mesh.shape["rep"]),
        mesh=mesh,
        in_specs=placed,
        out_specs=(P("section", "rep", None), P("section", "rep", None)),
        check_vma=False,
    )
```
